32 devices in a mesh: groups: 2 (over x), atom: 16 (over z, y, core).
Axes of the slice: x: 2, y: 2, z: 4, core: 2. Of those that a mesh axis runs over, the one named last changes fastest.
Arguments:
- atoms: float32 [128, 4096], P('atom'), may hold values from 0.2 to 2
- images: float32 [32, 16384], P(('groups', 'atom')), parts along dimension 0, may hold values from 0.2 to 2
- logits: float32 [32, 32], P(('groups', 'atom')), parts along dimension 0, may hold values from -4 to 4
Outputs:
- barycenters: float32 [32, 16384], P(('groups', 'atom')), parts along dimension 0
- atom_gradient: float32 [256, 4096], P(('groups', 'atom')), parts along dimension 0
The draws below stay inside these ranges and needn't reach their ends.
There are 2 independent parts, one for each index of `groups`. The reference program is written for one: setup_inputs(seed, part) draws one part's arguments, and reference() takes and returns one part's arrays. A program takes and returns all parts, laid end to end along the dimension named above; an argument that names none is the same for every part. Nothing has to cross between parts.
All inputs are finite; a program needn't handle non-finite values.
Results may differ from the reference program's by a relative error of at most 0.0001.
Values sent between devices are 32-bit elements; how exact they have to be, the bound alone decides.
A program may use at most 64 MiB of HBM per device.

```python
import math
import jax
import jax.numpy as jnp
from jax import lax

H = 128
W = 128
K = 32
HALF = 15
ITERS = 3
IMAGES = 16


def steps_of(own_key, extent, cuts, least, largest):
    def one(position, blocks):
        heights = jax.random.uniform(jax.random.fold_in(jax.random.fold_in(own_key, 6), position), (blocks,), jnp.float32, least / len(cuts), largest / len(cuts))
        return jnp.repeat(jnp.exp(heights), extent[position] // blocks).reshape((-1,) + (1,) * (len(extent) - position - 1))

    gain = one(*cuts[0])
    for cut in cuts[1:]:
        gain = gain * one(*cut)
    return gain


def normal_values(stream_key, dims, deviation, reach, cuts=(), kind=jnp.bfloat16):
    entries = jax.random.normal(stream_key, dims, jnp.float32) * deviation
    if len(cuts) > 0:
        entries = steps_of(stream_key, dims, cuts, -0.22, 0.18) * entries
    return jnp.clip(entries, min=-reach, max=reach).astype(kind)


def setup_inputs(seed: int = 0, part: int = 0) -> dict:
    streams_of = jax.random.split(jax.random.key(seed), 4)
    part_splits = jax.random.split(jax.random.fold_in(streams_of[3], part), 4)
    atoms = jnp.clip(jnp.exp(math.log(2.0) - 2.3025851 * jax.random.uniform(streams_of[0], (H, K * W), jnp.float32) ** steps_of(streams_of[0], (H, K * W), ((0, 16),), -0.2, 0.2)), 0.2, 2.0)
    images = jnp.clip(jnp.exp(math.log(2.0) - 2.3025851 * jax.random.uniform(part_splits[1], (IMAGES, H * W), jnp.float32) ** steps_of(part_splits[1], (IMAGES, H * W), ((0, 16),), -0.2, 0.2)), 0.2, 2.0)
    logits = normal_values(part_splits[2], (IMAGES, K), 1.0, 4.0, ((0, 16),), jnp.float32)
    return dict(atoms=atoms, images=images, logits=logits)


spread_squared = 50.0

def kernel_matrix(count):
    index = jnp.arange(count, dtype=jnp.float32)
    position_shift = index[:, None] - index[None, :]
    taps = jnp.arange(-HALF, HALF + 1, dtype=jnp.float32)
    total = jnp.sum(jnp.exp(-taps * taps / spread_squared))
    inside = jnp.abs(position_shift) <= HALF
    return jnp.where(inside, jnp.exp(-position_shift * position_shift / spread_squared), 0.0) / total

def blur_field(image_plane, row_kernel, column_kernel):
    spanning_devices = jnp.einsum('pbc,cd->pbd', image_plane, column_kernel, precision=lax.Precision.HIGHEST)
    return jnp.einsum('rn,nby->rby', row_kernel, spanning_devices, precision=lax.Precision.HIGHEST)

def barycenter(atoms3, first_blur, weights_img, row_kernel, column_kernel):
    blurred = first_blur
    scaling = None
    result = None
    for step_index in range(ITERS):
        if step_index > 0:
            back = blur_field(scaling, row_kernel, column_kernel)
            blurred = blur_field(atoms3 / back, row_kernel, column_kernel)
        logged = jnp.einsum('hkw,k->hw', jnp.log(blurred), weights_img, precision=lax.Precision.HIGHEST)
        result = jnp.exp(logged)
        scaling = result[:, None, :] / blurred
    return result

def reference(atoms, images, logits):
    row_kernel = kernel_matrix(H)
    column_kernel = kernel_matrix(W)
    atoms3 = atoms.reshape(H, K, W)
    ones_blur = lax.optimization_barrier(jnp.sum(row_kernel, axis=1))[:, None] * lax.optimization_barrier(jnp.sum(column_kernel, axis=0))[None, :]
    first_blur = blur_field(atoms3 / ones_blur[:, None, :], row_kernel, column_kernel)
    expo = jnp.exp(logits)
    weights_all = expo / lax.optimization_barrier(jnp.sum(expo, axis=1, keepdims=True))

    def one_image(carry, item):
        image_row, weights_img = item
        target = image_row.reshape(H, W)
        result, pullback = jax.vjp(lambda at, fb: barycenter(at, fb, weights_img, row_kernel, column_kernel), atoms3, first_blur)
        atoms_gradient, grad_first = pullback(result - target)
        return ((carry[0] + atoms_gradient, carry[1] + grad_first), result.reshape(H * W))
    start = (jnp.zeros((H, K, W), jnp.float32), jnp.zeros((H, K, W), jnp.float32))
    (atoms_gradient, grad_first), results = lax.scan(one_image, start, (images, weights_all))
    gradient = atoms_gradient + blur_field(grad_first, row_kernel, column_kernel) / ones_blur[:, None, :]
    return (results, gradient.reshape(H, K * W))
```

```python
import functools

import jax
import jax.numpy as jnp
import numpy as np
from jax import lax
from jax.experimental import pallas as pl
from jax.experimental.pallas import tpu as pltpu
from jax.sharding import PartitionSpec as P

K = 32
HALF = 15
SPREAD = 50.0
SLAB = 4

f32 = jnp.float32
bf16 = jnp.bfloat16


def split(x):
    hi = x.astype(bf16)
    lo = (x - hi.astype(f32)).astype(bf16)
    return hi, lo


def kernel_matrix(count):
    taps = np.arange(-HALF, HALF + 1, dtype=np.float64)
    total = float(np.sum(np.exp(-taps * taps / SPREAD)))
    i = lax.broadcasted_iota(jnp.int32, (count, count), 0)
    j = lax.broadcasted_iota(jnp.int32, (count, count), 1)
    d = (i - j).astype(f32)
    return jnp.where(jnp.abs(d) <= HALF, jnp.exp(d * d * (-1.0 / SPREAD)), 0.0) * (1.0 / total)


def kernel(H, W, a_ref, y_ref, logit_ref, p_ref, da_ref,
           wc, wr, re_ref, lam, rq1, rq2, rq3, rb2, rb3, u, p1, p2, acc, usum):
    gc = kernel_matrix(W)
    gr = kernel_matrix(H)
    ch, cl = split(gc)
    rh, rl = split(gr)
    wc[:W, :W] = ch
    wc[W:, :W] = ch
    wc[:W, W:] = cl
    wc[W:, W:] = jnp.zeros_like(cl)
    wr[:H, :H] = rh
    wr[:H, H:] = rh
    wr[H:, :H] = rl
    wr[H:, H:] = jnp.zeros_like(rl)
    re_ref[...] = 1.0 / (jnp.sum(gr, axis=1, keepdims=True) * jnp.sum(gc, axis=0, keepdims=True))
    e = jnp.exp(logit_ref[...])
    soft = e / jnp.sum(e, axis=1, keepdims=True)
    for k in range(K):
        lam[:, k * W:(k + 1) * W] = jnp.broadcast_to(soft[:, k:k + 1], (1, W))

    def blur(fields):
        left = []
        for x in fields:
            hi, lo = split(x)
            left.append(jnp.concatenate([hi, lo], axis=1))
        out = jnp.dot(jnp.concatenate(left, axis=0), wc[...], preferred_element_type=f32)
        out = out[:, :W] + out[:, W:]
        right = []
        for n in range(len(fields)):
            hi, lo = split(out[n * H:(n + 1) * H])
            right.append(jnp.concatenate([hi, lo], axis=0))
        out = jnp.dot(wr[...], jnp.concatenate(right, axis=1), preferred_element_type=f32)
        out = out[:H] + out[H:]
        return [out[:, n * W:(n + 1) * W] for n in range(len(fields))]

    def over_slabs(step):
        def one(s, carry):
            step([pl.ds(pl.multiple_of((s * SLAB + n) * W, W), W) for n in range(SLAB)])
            return carry
        lax.fori_loop(0, K // SLAB, one, 0)

    def add(total, parts):
        s = parts[0]
        for x in parts[1:]:
            s = s + x
        total[...] += s

    acc[...] = jnp.zeros_like(acc)

    def first(cols):
        q = blur([a_ref[:, c] * re_ref[...] for c in cols])
        for c, x in zip(cols, q):
            rq1[:, c] = 1.0 / x
        add(acc, [lam[:, c] * jnp.log(x) for c, x in zip(cols, q)])
    over_slabs(first)

    def forward(p, rq_in, rb, rq_out):
        p[...] = jnp.exp(acc[...])
        acc[...] = jnp.zeros_like(acc)

        def step(cols):
            b = blur([p[...] * rq_in[:, c] for c in cols])
            r = []
            for c, x in zip(cols, b):
                inv = 1.0 / x
                rb[:, c] = inv
                r.append(a_ref[:, c] * inv)
            q = blur(r)
            for c, x in zip(cols, q):
                rq_out[:, c] = 1.0 / x
            add(acc, [lam[:, c] * jnp.log(x) for c, x in zip(cols, q)])
        over_slabs(step)

    forward(p1, rq1, rb2, rq2)
    forward(p2, rq2, rb3, rq3)
    result = jnp.exp(acc[...])
    p_ref[...] = result
    acc[...] = (y_ref[...] - result) * result

    def backward(p, rq, rb, rq_before, newest):
        usum[...] = acc[...]
        acc[...] = jnp.zeros_like(acc)

        def step(cols):
            dq = []
            for c in cols:
                g = lam[:, c] * usum[...]
                g = -g if newest else u[:, c] - g
                dq.append(g * rq[:, c])
            dr = blur(dq)
            db = []
            for c, x in zip(cols, dr):
                inv = rb[:, c]
                t = x * inv
                if newest:
                    da_ref[:, c] = t
                else:
                    da_ref[:, c] += t
                db.append(t * (a_ref[:, c] * inv))
            dv = blur(db)
            parts = []
            for c, x in zip(cols, dv):
                x = x * (p[...] * rq_before[:, c])
                u[:, c] = x
                parts.append(x)
            add(acc, parts)
        over_slabs(step)

    backward(p2, rq3, rb3, rq2, True)
    backward(p1, rq2, rb2, rq1, False)
    usum[...] = acc[...]

    def last(cols):
        d = blur([(u[:, c] - lam[:, c] * usum[...]) * rq1[:, c] for c in cols])
        for c, x in zip(cols, d):
            da_ref[:, c] += x * re_ref[...]
    over_slabs(last)


def body(atoms, images, logits, *, parts):
    rows, wide = atoms.shape
    H, W = rows * parts, wide // K
    gathered = lax.all_gather(atoms, "atom", axis=0, tiled=True)
    field = pltpu.VMEM((H, wide), f32)
    plane = pltpu.VMEM((H, W), f32)
    call = pl.pallas_call(
        functools.partial(kernel, H, W),
        out_shape=(jax.ShapeDtypeStruct((H, W), f32), jax.ShapeDtypeStruct((H, wide), f32)),
        in_specs=[pl.BlockSpec(memory_space=pltpu.VMEM)] * 3,
        out_specs=[pl.BlockSpec(memory_space=pltpu.VMEM)] * 2,
        scratch_shapes=[
            pltpu.VMEM((2 * W, 2 * W), bf16),
            pltpu.VMEM((2 * H, 2 * H), bf16),
            plane,
            pltpu.VMEM((1, wide), f32),
            field, field, field, field, field, field,
            plane, plane, plane, plane,
        ],
        compiler_params=pltpu.CompilerParams(vmem_limit_bytes=40 * 2**20),
    )
    results, grads = [], []
    for n in range(images.shape[0]):
        p, da = call(gathered, images[n].reshape(H, W), logits[n:n + 1])
        results.append(p.reshape(1, H * W))
        grads.append(da)
    result = results[0] if len(results) == 1 else jnp.concatenate(results, axis=0)
    term = sum(grads[1:], grads[0])
    return result, lax.psum_scatter(term, "atom", scatter_dimension=0, tiled=True)


def solution(mesh):
    return jax.shard_map(
        functools.partial(body, parts=mesh.shape["atom"]),
        mesh=mesh,
        in_specs=(P("atom", None), P(("groups", "atom"), None), P(("groups", "atom"), None)),
        out_specs=(P(("groups", "atom"), None), P(("groups", "atom"), None)),
        check_vma=False,
    )
```

```python
import functools

import jax
import jax.numpy as jnp
import numpy as np
from jax import lax
from jax.experimental import pallas as pl
from jax.experimental.pallas import tpu as pltpu
from jax.sharding import PartitionSpec as P

K = 32
HALF = 15
SPREAD = 50.0
SLAB = 4
CHUNKS = 4

f32 = jnp.float32
bf16 = jnp.bfloat16


def split(x):
    hi = x.astype(bf16)
    lo = (x - hi.astype(f32)).astype(bf16)
    return hi, lo


def kernel_matrix(count):
    taps = np.arange(-HALF, HALF + 1, dtype=np.float64)
    total = float(np.sum(np.exp(-taps * taps / SPREAD)))
    i = lax.broadcasted_iota(jnp.int32, (count, count), 0)
    j = lax.broadcasted_iota(jnp.int32, (count, count), 1)
    d = (i - j).astype(f32)
    return jnp.where(jnp.abs(d) <= HALF, jnp.exp(d * d * (-1.0 / SPREAD)), 0.0) * (1.0 / total)


def chip_grid(parts):
    chips = parts // 2
    ny = 2 ** ((chips.bit_length() - 1) // 2)
    return chips // ny, ny


class Links:
    def __init__(self, parts, rows, x_ref, out_ref, a_ref, da_ref, rc, sy, ry, keep, sz, rz, sems):
        self.nz, self.ny = chip_grid(parts)
        self.rows = rows
        self.x_ref, self.out_ref, self.a_ref, self.da_ref = x_ref, out_ref, a_ref, da_ref
        self.rc, self.sy, self.ry, self.keep, self.sz, self.rz = rc, sy, ry, keep, sz, rz
        self.sems = sems
        me = lax.axis_index("atom")
        self.me = me
        self.c = lax.rem(me, 2)
        self.y = lax.rem(me // 2, self.ny)
        self.z = me // (2 * self.ny)
        self.width = a_ref.shape[1] // CHUNKS
        self.sent = []
        self.live = {}

    def index(self, z, y, c):
        return (z * self.ny + y) * 2 + c

    def zp(self, d):
        return lax.rem(self.z + d, self.nz)

    def zm(self, d):
        return lax.rem(self.z + self.nz - d, self.nz)

    def yp(self, d):
        return lax.rem(self.y + d, self.ny)

    def ym(self, d):
        return lax.rem(self.y + self.ny - d, self.ny)

    def barrier(self):
        bar = pltpu.get_barrier_semaphore()
        peers = [self.index(self.z, self.y, 1 - self.c)]
        peers += [self.index(self.zp(d), self.y, self.c) for d in range(1, self.nz)]
        peers += [self.index(self.z, self.yp(d), self.c) for d in range(1, self.ny)]
        for peer in peers:
            pl.semaphore_signal(bar, inc=1, device_id={"atom": peer}, device_id_type=pl.DeviceIdType.MESH)
        pl.semaphore_wait(bar, len(peers))

    def send(self, key, number, src, dst, peer):
        send, recv = self.sems
        copy = pltpu.make_async_remote_copy(
            src_ref=src, dst_ref=dst, send_sem=send.at[number], recv_sem=recv.at[number],
            device_id={"atom": peer}, device_id_type=pl.DeviceIdType.MESH)
        copy.start()
        self.live[key] = copy
        self.sent.append(copy)

    def arrived(self, key):
        self.live[key].wait_recv()

    def finish(self):
        for copy in self.sent:
            copy.wait_send()

    def cols(self, j):
        return pl.ds(j * self.width, self.width)

    def shard(self, index, j):
        return self.a_ref.at[pl.ds(pl.multiple_of(index * self.rows, self.rows), self.rows), self.cols(j)]

    def slots(self):
        return (self.nz - 1) + (self.ny - 1) * self.nz + self.nz * self.ny

    def pass_on(self, what, number, index, j, peer):
        ref = self.shard(index, j)
        self.send((what, number, j), j * self.slots() + number, ref, ref, peer)

    def sibling(self):
        return self.index(self.z, self.y, 1 - self.c)

    def gather_start(self):
        self.a_ref[pl.ds(pl.multiple_of(self.me * self.rows, self.rows), self.rows), :] = self.x_ref[...]
        for j in range(CHUNKS):
            for d in range(1, self.nz):
                self.pass_on("g", d - 1, self.me, j, self.index(self.zp(d), self.y, self.c))
            self.spread(0, j)

    def spread(self, dz, j):
        index = self.index(self.zm(dz), self.y, self.c)
        for dy in range(1, self.ny):
            self.pass_on("g", (self.nz - 1) + (dy - 1) * self.nz + dz, index, j, self.index(self.z, self.yp(dy), self.c))
        self.pass_on("g", (self.nz - 1) + (self.ny - 1) * self.nz + dz, index, j, self.sibling())

    def gather_z(self, j):
        for dz in range(1, self.nz):
            self.arrived(("g", dz - 1, j))
            self.spread(dz, j)

    def gather_y(self, j):
        base = (self.nz - 1) + (self.ny - 1) * self.nz
        for dy in range(1, self.ny):
            for dz in range(self.nz):
                self.arrived(("g", (self.nz - 1) + (dy - 1) * self.nz + dz, j))
                index = self.index(self.zm(dz), self.ym(dy), self.c)
                self.pass_on("g", base + dy * self.nz + dz, index, j, self.sibling())

    def gather_done(self, j):
        base = (self.nz - 1) + (self.ny - 1) * self.nz
        for n in range(self.nz * self.ny):
            self.arrived(("g", base + n, j))

    def number(self, j, slot):
        return CHUNKS * self.slots() + j * (1 + (self.ny - 1) + (self.nz - 1)) + slot

    def reduce_core(self, j):
        cols = self.cols(j)
        self.send(("c", j), self.number(j, 0), self.da_ref.at[:, 1 - self.c, :, cols],
                  self.rc.at[:, :, cols], self.sibling())

    def reduce_y(self, j):
        cols = self.cols(j)
        self.arrived(("c", j))
        for dy in range(self.ny):
            y = self.yp(dy)
            for z in range(self.nz):
                chip = z * self.ny + y
                total = self.da_ref[chip, self.c, :, cols] + self.rc[chip, :, cols]
                if dy == 0:
                    self.keep[z, :, cols] = total
                else:
                    self.sy[dy - 1, z, :, cols] = total
            if dy > 0:
                self.send(("y", dy, j), self.number(j, dy), self.sy.at[dy - 1, :, :, cols],
                          self.ry.at[dy - 1, :, :, cols], self.index(self.z, y, self.c))

    def reduce_z(self, j):
        cols = self.cols(j)
        for dy in range(1, self.ny):
            self.arrived(("y", dy, j))
        for dz in [*range(1, self.nz), 0]:
            z = self.zp(dz)
            total = self.keep[z, :, cols]
            for dy in range(1, self.ny):
                total = total + self.ry[dy - 1, z, :, cols]
            if dz == 0:
                self.out_ref[:, cols] = total
            else:
                self.sz[dz - 1, :, cols] = total
                self.send(("z", dz, j), self.number(j, self.ny - 1 + dz), self.sz.at[dz - 1, :, cols],
                          self.rz.at[dz - 1, :, cols], self.index(z, self.y, self.c))

    def reduce_done(self, j):
        cols = self.cols(j)
        total = self.out_ref[:, cols]
        for dz in range(1, self.nz):
            self.arrived(("z", dz, j))
            total = total + self.rz[dz - 1, :, cols]
        self.out_ref[:, cols] = total


def kernel(H, W, parts, linked, x_ref, y_ref, logit_ref, p_ref, out_ref,
           wc, wr, re_ref, lam, rq1, rq2, rq3, rb2, rb3, u, p1, p2, acc, usum, *rest):
    if linked:
        a_ref, da_ref = rest[:2]
        links = Links(parts, H // parts, x_ref, out_ref, a_ref, da_ref, *rest[2:8], rest[8:10])
        links.barrier()
        links.gather_start()

        def get_da(c):
            return da_ref[:, :, :, c].reshape(H, W)

        def set_da(c, value):
            da_ref[:, :, :, c] = value.reshape(parts // 2, 2, H // parts, W)
    else:
        a_ref = x_ref

        def get_da(c):
            return out_ref[:, c]

        def set_da(c, value):
            out_ref[:, c] = value

    gc = kernel_matrix(W)
    gr = kernel_matrix(H)
    ch, cl = split(gc)
    rh, rl = split(gr)
    wc[:W, :W] = ch
    wc[W:, :W] = ch
    wc[:W, W:] = cl
    wc[W:, W:] = jnp.zeros_like(cl)
    wr[:H, :H] = rh
    wr[:H, H:] = rh
    wr[H:, :H] = rl
    wr[H:, H:] = jnp.zeros_like(rl)
    re_ref[...] = 1.0 / (jnp.sum(gr, axis=1, keepdims=True) * jnp.sum(gc, axis=0, keepdims=True))
    e = jnp.exp(logit_ref[...])
    soft = e / jnp.sum(e, axis=1, keepdims=True)
    for k in range(K):
        lam[:, k * W:(k + 1) * W] = jnp.broadcast_to(soft[:, k:k + 1], (1, W))

    def blur(fields):
        left = []
        for x in fields:
            hi, lo = split(x)
            left.append(jnp.concatenate([hi, lo], axis=1))
        out = jnp.dot(jnp.concatenate(left, axis=0), wc[...], preferred_element_type=f32)
        out = out[:, :W] + out[:, W:]
        right = []
        for n in range(len(fields)):
            hi, lo = split(out[n * H:(n + 1) * H])
            right.append(jnp.concatenate([hi, lo], axis=0))
        out = jnp.dot(wr[...], jnp.concatenate(right, axis=1), preferred_element_type=f32)
        out = out[:H] + out[H:]
        return [out[:, n * W:(n + 1) * W] for n in range(len(fields))]

    def over_slabs(step, begin=0, end=K):
        def one(s, carry):
            step([pl.ds(pl.multiple_of((s * SLAB + n) * W, W), W) for n in range(SLAB)])
            return carry
        lax.fori_loop(begin // SLAB, end // SLAB, one, 0)

    def over_chunk(step, j):
        over_slabs(step, j * K // CHUNKS, (j + 1) * K // CHUNKS)

    def add(total, parts):
        s = parts[0]
        for x in parts[1:]:
            s = s + x
        total[...] += s

    acc[...] = jnp.zeros_like(acc)

    def first(cols):
        q = blur([a_ref[:, c] * re_ref[...] for c in cols])
        for c, x in zip(cols, q):
            rq1[:, c] = 1.0 / x
        add(acc, [lam[:, c] * jnp.log(x) for c, x in zip(cols, q)])
    if linked:
        for t in range(CHUNKS + 2):
            if t < CHUNKS:
                links.gather_z(t)
            if 0 <= t - 1 < CHUNKS:
                links.gather_y(t - 1)
            if t >= 2:
                links.gather_done(t - 2)
                over_chunk(first, t - 2)
    else:
        over_slabs(first)

    def forward(p, rq_in, rb, rq_out):
        p[...] = jnp.exp(acc[...])
        acc[...] = jnp.zeros_like(acc)

        def step(cols):
            b = blur([p[...] * rq_in[:, c] for c in cols])
            r = []
            for c, x in zip(cols, b):
                inv = 1.0 / x
                rb[:, c] = inv
                r.append(a_ref[:, c] * inv)
            q = blur(r)
            for c, x in zip(cols, q):
                rq_out[:, c] = 1.0 / x
            add(acc, [lam[:, c] * jnp.log(x) for c, x in zip(cols, q)])
        over_slabs(step)

    forward(p1, rq1, rb2, rq2)
    forward(p2, rq2, rb3, rq3)
    result = jnp.exp(acc[...])
    p_ref[...] = result
    acc[...] = (y_ref[...] - result) * result

    def backward(p, rq, rb, rq_before, newest):
        usum[...] = acc[...]
        acc[...] = jnp.zeros_like(acc)

        def step(cols):
            dq = []
            for c in cols:
                g = lam[:, c] * usum[...]
                g = -g if newest else u[:, c] - g
                dq.append(g * rq[:, c])
            dr = blur(dq)
            db = []
            for c, x in zip(cols, dr):
                inv = rb[:, c]
                t = x * inv
                set_da(c, t if newest else get_da(c) + t)
                db.append(t * (a_ref[:, c] * inv))
            dv = blur(db)
            parts = []
            for c, x in zip(cols, dv):
                x = x * (p[...] * rq_before[:, c])
                u[:, c] = x
                parts.append(x)
            add(acc, parts)
        over_slabs(step)

    backward(p2, rq3, rb3, rq2, True)
    backward(p1, rq2, rb2, rq1, False)
    usum[...] = acc[...]

    def last(cols):
        d = blur([(u[:, c] - lam[:, c] * usum[...]) * rq1[:, c] for c in cols])
        for c, x in zip(cols, d):
            set_da(c, get_da(c) + x * re_ref[...])
    if linked:
        for t in range(CHUNKS + 3):
            if t < CHUNKS:
                over_chunk(last, t)
                links.reduce_core(t)
            if 0 <= t - 1 < CHUNKS:
                links.reduce_y(t - 1)
            if 0 <= t - 2 < CHUNKS:
                links.reduce_z(t - 2)
            if t >= 3:
                links.reduce_done(t - 3)
        links.finish()
    else:
        over_slabs(last)


def body(atoms, images, logits, *, parts):
    rows, wide = atoms.shape
    H, W = rows * parts, wide // K
    linked = rows % 8 == 0 and images.shape[0] == 1 and parts % 2 == 0
    field = pltpu.VMEM((H, wide), f32)
    plane = pltpu.VMEM((H, W), f32)
    scratch = [
        pltpu.VMEM((2 * W, 2 * W), bf16),
        pltpu.VMEM((2 * H, 2 * H), bf16),
        plane,
        pltpu.VMEM((1, wide), f32),
        field, field, field, field, field, field,
        plane, plane, plane, plane,
    ]
    extra = {}
    if linked:
        nz, ny = chip_grid(parts)
        copies = CHUNKS * ((nz - 1) + (ny - 1) * nz + nz * ny + 1 + (ny - 1) + (nz - 1))
        scratch += [
            field,
            pltpu.VMEM((nz * ny, 2, rows, wide), f32),
            pltpu.VMEM((nz * ny, rows, wide), f32),
            pltpu.VMEM((max(ny - 1, 1), nz, rows, wide), f32),
            pltpu.VMEM((max(ny - 1, 1), nz, rows, wide), f32),
            pltpu.VMEM((nz, rows, wide), f32),
            pltpu.VMEM((max(nz - 1, 1), rows, wide), f32),
            pltpu.VMEM((max(nz - 1, 1), rows, wide), f32),
            pltpu.SemaphoreType.DMA((copies,)),
            pltpu.SemaphoreType.DMA((copies,)),
        ]
        extra = dict(collective_id=0, has_side_effects=True)
    call = pl.pallas_call(
        functools.partial(kernel, H, W, parts, linked),
        out_shape=(
            jax.ShapeDtypeStruct((H, W), f32),
            jax.ShapeDtypeStruct((rows if linked else H, wide), f32),
        ),
        in_specs=[pl.BlockSpec(memory_space=pltpu.VMEM)] * 3,
        out_specs=[pl.BlockSpec(memory_space=pltpu.VMEM)] * 2,
        scratch_shapes=scratch,
        compiler_params=pltpu.CompilerParams(vmem_limit_bytes=44 * 2**20, **extra),
    )
    if linked:
        p, da = call(atoms, images.reshape(H, W), logits)
        return p.reshape(1, H * W), da
    gathered = lax.all_gather(atoms, "atom", axis=0, tiled=True)
    results, grads = [], []
    for n in range(images.shape[0]):
        p, da = call(gathered, images[n].reshape(H, W), logits[n:n + 1])
        results.append(p.reshape(1, H * W))
        grads.append(da)
    result = results[0] if len(results) == 1 else jnp.concatenate(results, axis=0)
    term = sum(grads[1:], grads[0])
    return result, lax.psum_scatter(term, "atom", scatter_dimension=0, tiled=True)


def solution(mesh):
    return jax.shard_map(
        functools.partial(body, parts=mesh.shape["atom"]),
        mesh=mesh,
        in_specs=(P("atom", None), P(("groups", "atom"), None), P(("groups", "atom"), None)),
        out_specs=(P(("groups", "atom"), None), P(("groups", "atom"), None)),
        check_vma=False,
    )
```

```python
import functools

import jax
import jax.numpy as jnp
import numpy as np
from jax import lax
from jax.experimental import pallas as pl
from jax.experimental.pallas import tpu as pltpu
from jax.sharding import PartitionSpec as P

K = 32
HALF = 15
SPREAD = 50.0
SLAB = 16
CHUNKS = 2

f32 = jnp.float32
bf16 = jnp.bfloat16


def split(x):
    hi = x.astype(bf16)
    lo = (x - hi.astype(f32)).astype(bf16)
    return hi, lo


def kernel_matrix(count):
    taps = np.arange(-HALF, HALF + 1, dtype=np.float64)
    total = float(np.sum(np.exp(-taps * taps / SPREAD)))
    i = lax.broadcasted_iota(jnp.int32, (count, count), 0)
    j = lax.broadcasted_iota(jnp.int32, (count, count), 1)
    d = (i - j).astype(f32)
    return jnp.where(jnp.abs(d) <= HALF, jnp.exp(d * d * (-1.0 / SPREAD)), 0.0) * (1.0 / total)


def chip_grid(parts):
    chips = parts // 2
    ny = 2 ** ((chips.bit_length() - 1) // 2)
    return chips // ny, ny


class Links:
    def __init__(self, parts, rows, x_ref, out_ref, a_ref, da_ref, rc, sy, ry, keep, sz, rz, sems):
        self.nz, self.ny = chip_grid(parts)
        self.rows = rows
        self.x_ref, self.out_ref, self.a_ref, self.da_ref = x_ref, out_ref, a_ref, da_ref
        self.rc, self.sy, self.ry, self.keep, self.sz, self.rz = rc, sy, ry, keep, sz, rz
        self.sems = sems
        me = lax.axis_index("atom")
        self.me = me
        self.c = lax.rem(me, 2)
        self.y = lax.rem(me // 2, self.ny)
        self.z = me // (2 * self.ny)
        self.width = a_ref.shape[1] // CHUNKS
        self.sent = []
        self.live = {}

    def index(self, z, y, c):
        return (z * self.ny + y) * 2 + c

    def zp(self, d):
        return lax.rem(self.z + d, self.nz)

    def zm(self, d):
        return lax.rem(self.z + self.nz - d, self.nz)

    def yp(self, d):
        return lax.rem(self.y + d, self.ny)

    def ym(self, d):
        return lax.rem(self.y + self.ny - d, self.ny)

    def barrier(self):
        bar = pltpu.get_barrier_semaphore()
        peers = [self.index(self.z, self.y, 1 - self.c)]
        peers += [self.index(self.zp(d), self.y, self.c) for d in range(1, self.nz)]
        peers += [self.index(self.z, self.yp(d), self.c) for d in range(1, self.ny)]
        for peer in peers:
            pl.semaphore_signal(bar, inc=1, device_id={"atom": peer}, device_id_type=pl.DeviceIdType.MESH)
        pl.semaphore_wait(bar, len(peers))

    def send(self, key, number, src, dst, peer):
        send, recv = self.sems
        copy = pltpu.make_async_remote_copy(
            src_ref=src, dst_ref=dst, send_sem=send.at[number], recv_sem=recv.at[number],
            device_id={"atom": peer}, device_id_type=pl.DeviceIdType.MESH)
        copy.start()
        self.live[key] = copy
        self.sent.append(copy)

    def arrived(self, key):
        self.live[key].wait_recv()

    def finish(self):
        for copy in self.sent:
            copy.wait_send()

    def cols(self, j):
        return pl.ds(j * self.width, self.width)

    def shard(self, index, j):
        return self.a_ref.at[pl.ds(pl.multiple_of(index * self.rows, self.rows), self.rows), self.cols(j)]

    def slots(self):
        return (self.nz - 1) + (self.ny - 1) * self.nz + self.nz * self.ny

    def pass_on(self, what, number, index, j, peer):
        ref = self.shard(index, j)
        self.send((what, number, j), j * self.slots() + number, ref, ref, peer)

    def sibling(self):
        return self.index(self.z, self.y, 1 - self.c)

    def gather_start(self):
        self.a_ref[pl.ds(pl.multiple_of(self.me * self.rows, self.rows), self.rows), :] = self.x_ref[...]
        for j in range(CHUNKS):
            for d in range(1, self.nz):
                self.pass_on("g", d - 1, self.me, j, self.index(self.zp(d), self.y, self.c))
            self.spread(0, j)

    def spread(self, dz, j):
        index = self.index(self.zm(dz), self.y, self.c)
        for dy in range(1, self.ny):
            self.pass_on("g", (self.nz - 1) + (dy - 1) * self.nz + dz, index, j, self.index(self.z, self.yp(dy), self.c))
        self.pass_on("g", (self.nz - 1) + (self.ny - 1) * self.nz + dz, index, j, self.sibling())

    def gather_z(self, j):
        for dz in range(1, self.nz):
            self.arrived(("g", dz - 1, j))
            self.spread(dz, j)

    def gather_y(self, j):
        base = (self.nz - 1) + (self.ny - 1) * self.nz
        for dy in range(1, self.ny):
            for dz in range(self.nz):
                self.arrived(("g", (self.nz - 1) + (dy - 1) * self.nz + dz, j))
                index = self.index(self.zm(dz), self.ym(dy), self.c)
                self.pass_on("g", base + dy * self.nz + dz, index, j, self.sibling())

    def gather_done(self, j):
        base = (self.nz - 1) + (self.ny - 1) * self.nz
        for n in range(self.nz * self.ny):
            self.arrived(("g", base + n, j))

    def number(self, j, slot):
        return CHUNKS * self.slots() + j * (1 + (self.ny - 1) + (self.nz - 1)) + slot

    def reduce_core(self, j):
        cols = self.cols(j)
        self.send(("c", j), self.number(j, 0), self.da_ref.at[:, 1 - self.c, :, cols],
                  self.rc.at[:, :, cols], self.sibling())

    def reduce_y(self, j):
        cols = self.cols(j)
        self.arrived(("c", j))
        for dy in range(self.ny):
            y = self.yp(dy)
            for z in range(self.nz):
                chip = z * self.ny + y
                total = self.da_ref[chip, self.c, :, cols] + self.rc[chip, :, cols]
                if dy == 0:
                    self.keep[z, :, cols] = total
                else:
                    self.sy[dy - 1, z, :, cols] = total
            if dy > 0:
                self.send(("y", dy, j), self.number(j, dy), self.sy.at[dy - 1, :, :, cols],
                          self.ry.at[dy - 1, :, :, cols], self.index(self.z, y, self.c))

    def reduce_z(self, j):
        cols = self.cols(j)
        for dy in range(1, self.ny):
            self.arrived(("y", dy, j))
        for dz in [*range(1, self.nz), 0]:
            z = self.zp(dz)
            total = self.keep[z, :, cols]
            for dy in range(1, self.ny):
                total = total + self.ry[dy - 1, z, :, cols]
            if dz == 0:
                self.out_ref[:, cols] = total
            else:
                self.sz[dz - 1, :, cols] = total
                self.send(("z", dz, j), self.number(j, self.ny - 1 + dz), self.sz.at[dz - 1, :, cols],
                          self.rz.at[dz - 1, :, cols], self.index(z, self.y, self.c))

    def reduce_done(self, j):
        cols = self.cols(j)
        total = self.out_ref[:, cols]
        for dz in range(1, self.nz):
            self.arrived(("z", dz, j))
            total = total + self.rz[dz - 1, :, cols]
        self.out_ref[:, cols] = total


def kernel(H, W, parts, linked, x_ref, y_ref, logit_ref, p_ref, out_ref,
           wc, wr, re_ref, lam, rq1, rq2, rq3, rb2, rb3, u, p1, p2, acc, usum, *rest):
    if linked:
        a_ref, da_ref = rest[:2]
        links = Links(parts, H // parts, x_ref, out_ref, a_ref, da_ref, *rest[2:8], rest[8:10])
        links.barrier()
        links.gather_start()

        def get_da(c):
            return da_ref[:, :, :, c].reshape(H, W)

        def set_da(c, value):
            da_ref[:, :, :, c] = value.reshape(parts // 2, 2, H // parts, W)
    else:
        a_ref = x_ref

        def get_da(c):
            return out_ref[:, c]

        def set_da(c, value):
            out_ref[:, c] = value

    gc = kernel_matrix(W)
    gr = kernel_matrix(H)
    ch, cl = split(gc)
    rh, rl = split(gr)
    wc[:W, :W] = ch
    wc[W:, :W] = ch
    wc[:W, W:] = cl
    wc[W:, W:] = jnp.zeros_like(cl)
    wr[:H, :H] = rh
    wr[:H, H:] = rh
    wr[H:, :H] = rl
    wr[H:, H:] = jnp.zeros_like(rl)
    re_ref[...] = 1.0 / (jnp.sum(gr, axis=1, keepdims=True) * jnp.sum(gc, axis=0, keepdims=True))
    e = jnp.exp(logit_ref[...])
    soft = e / jnp.sum(e, axis=1, keepdims=True)
    for k in range(K):
        lam[:, k * W:(k + 1) * W] = jnp.broadcast_to(soft[:, k:k + 1], (1, W))

    def blur(fields):
        left = []
        for x in fields:
            hi, lo = split(x)
            left.append(jnp.concatenate([hi, lo], axis=1))
        out = jnp.dot(jnp.concatenate(left, axis=0), wc[...], preferred_element_type=f32)
        out = out[:, :W] + out[:, W:]
        right = []
        for n in range(len(fields)):
            hi, lo = split(out[n * H:(n + 1) * H])
            right.append(jnp.concatenate([hi, lo], axis=0))
        out = jnp.dot(wr[...], jnp.concatenate(right, axis=1), preferred_element_type=f32)
        out = out[:H] + out[H:]
        return [out[:, n * W:(n + 1) * W] for n in range(len(fields))]

    def over_slabs(step, begin=0, end=K):
        def one(s, carry):
            step([pl.ds(pl.multiple_of((s * SLAB + n) * W, W), W) for n in range(SLAB)])
            return carry
        lax.fori_loop(begin // SLAB, end // SLAB, one, 0)

    def over_chunk(step, j):
        over_slabs(step, j * K // CHUNKS, (j + 1) * K // CHUNKS)

    def add(total, parts):
        s = parts[0]
        for x in parts[1:]:
            s = s + x
        total[...] += s

    acc[...] = jnp.zeros_like(acc)

    def first(cols):
        q = blur([a_ref[:, c] * re_ref[...] for c in cols])
        for c, x in zip(cols, q):
            rq1[:, c] = 1.0 / x
        add(acc, [lam[:, c] * jnp.log(x) for c, x in zip(cols, q)])
    if linked:
        for t in range(CHUNKS + 2):
            if t < CHUNKS:
                links.gather_z(t)
            if 0 <= t - 1 < CHUNKS:
                links.gather_y(t - 1)
            if t >= 2:
                links.gather_done(t - 2)
                over_chunk(first, t - 2)
    else:
        over_slabs(first)

    def forward(p, rq_in, rb, rq_out):
        p[...] = jnp.exp(acc[...])
        acc[...] = jnp.zeros_like(acc)

        def step(cols):
            b = blur([p[...] * rq_in[:, c] for c in cols])
            r = []
            for c, x in zip(cols, b):
                inv = 1.0 / x
                rb[:, c] = inv
                r.append(a_ref[:, c] * inv)
            q = blur(r)
            for c, x in zip(cols, q):
                rq_out[:, c] = 1.0 / x
            add(acc, [lam[:, c] * jnp.log(x) for c, x in zip(cols, q)])
        over_slabs(step)

    forward(p1, rq1, rb2, rq2)
    forward(p2, rq2, rb3, rq3)
    result = jnp.exp(acc[...])
    p_ref[...] = result
    acc[...] = (y_ref[...] - result) * result

    def backward(p, rq, rb, rq_before, newest):
        usum[...] = acc[...]
        acc[...] = jnp.zeros_like(acc)

        def step(cols):
            dq = []
            for c in cols:
                g = lam[:, c] * usum[...]
                g = -g if newest else u[:, c] - g
                dq.append(g * rq[:, c])
            dr = blur(dq)
            db = []
            for c, x in zip(cols, dr):
                inv = rb[:, c]
                t = x * inv
                set_da(c, t if newest else get_da(c) + t)
                db.append(t * (a_ref[:, c] * inv))
            dv = blur(db)
            parts = []
            for c, x in zip(cols, dv):
                x = x * (p[...] * rq_before[:, c])
                u[:, c] = x
                parts.append(x)
            add(acc, parts)
        over_slabs(step)

    backward(p2, rq3, rb3, rq2, True)
    backward(p1, rq2, rb2, rq1, False)
    usum[...] = acc[...]

    def last(cols):
        d = blur([(u[:, c] - lam[:, c] * usum[...]) * rq1[:, c] for c in cols])
        for c, x in zip(cols, d):
            set_da(c, get_da(c) + x * re_ref[...])
    if linked:
        for t in range(CHUNKS + 3):
            if t < CHUNKS:
                over_chunk(last, t)
                links.reduce_core(t)
            if 0 <= t - 1 < CHUNKS:
                links.reduce_y(t - 1)
            if 0 <= t - 2 < CHUNKS:
                links.reduce_z(t - 2)
            if t >= 3:
                links.reduce_done(t - 3)
        links.finish()
    else:
        over_slabs(last)


def body(atoms, images, logits, *, parts):
    rows, wide = atoms.shape
    H, W = rows * parts, wide // K
    linked = rows % 8 == 0 and images.shape[0] == 1 and parts % 2 == 0
    field = pltpu.VMEM((H, wide), f32)
    plane = pltpu.VMEM((H, W), f32)
    scratch = [
        pltpu.VMEM((2 * W, 2 * W), bf16),
        pltpu.VMEM((2 * H, 2 * H), bf16),
        plane,
        pltpu.VMEM((1, wide), f32),
        field, field, field, field, field, field,
        plane, plane, plane, plane,
    ]
    extra = {}
    if linked:
        nz, ny = chip_grid(parts)
        copies = CHUNKS * ((nz - 1) + (ny - 1) * nz + nz * ny + 1 + (ny - 1) + (nz - 1))
        scratch += [
            field,
            pltpu.VMEM((nz * ny, 2, rows, wide), f32),
            pltpu.VMEM((nz * ny, rows, wide), f32),
            pltpu.VMEM((max(ny - 1, 1), nz, rows, wide), f32),
            pltpu.VMEM((max(ny - 1, 1), nz, rows, wide), f32),
            pltpu.VMEM((nz, rows, wide), f32),
            pltpu.VMEM((max(nz - 1, 1), rows, wide), f32),
            pltpu.VMEM((max(nz - 1, 1), rows, wide), f32),
            pltpu.SemaphoreType.DMA((copies,)),
            pltpu.SemaphoreType.DMA((copies,)),
        ]
        extra = dict(collective_id=0, has_side_effects=True)
    call = pl.pallas_call(
        functools.partial(kernel, H, W, parts, linked),
        out_shape=(
            jax.ShapeDtypeStruct((H, W), f32),
            jax.ShapeDtypeStruct((rows if linked else H, wide), f32),
        ),
        in_specs=[pl.BlockSpec(memory_space=pltpu.VMEM)] * 3,
        out_specs=[pl.BlockSpec(memory_space=pltpu.VMEM)] * 2,
        scratch_shapes=scratch,
        compiler_params=pltpu.CompilerParams(vmem_limit_bytes=44 * 2**20, **extra),
    )
    if linked:
        p, da = call(atoms, images.reshape(H, W), logits)
        return p.reshape(1, H * W), da
    gathered = lax.all_gather(atoms, "atom", axis=0, tiled=True)
    results, grads = [], []
    for n in range(images.shape[0]):
        p, da = call(gathered, images[n].reshape(H, W), logits[n:n + 1])
        results.append(p.reshape(1, H * W))
        grads.append(da)
    result = results[0] if len(results) == 1 else jnp.concatenate(results, axis=0)
    term = sum(grads[1:], grads[0])
    return result, lax.psum_scatter(term, "atom", scatter_dimension=0, tiled=True)


def solution(mesh):
    return jax.shard_map(
        functools.partial(body, parts=mesh.shape["atom"]),
        mesh=mesh,
        in_specs=(P("atom", None), P(("groups", "atom"), None), P(("groups", "atom"), None)),
        out_specs=(P(("groups", "atom"), None), P(("groups", "atom"), None)),
        check_vma=False,
    )
```

```python
import functools

import jax
import jax.numpy as jnp
import numpy as np
from jax import lax
from jax.experimental import pallas as pl
from jax.experimental.pallas import tpu as pltpu
from jax.sharding import PartitionSpec as P

K = 32
HALF = 15
SPREAD = 50.0
SLAB = 16
CHUNKS = 2

f32 = jnp.float32
bf16 = jnp.bfloat16


def split(x):
    hi = x.astype(bf16)
    lo = (x - hi.astype(f32)).astype(bf16)
    return hi, lo


def kernel_matrix(count):
    taps = np.arange(-HALF, HALF + 1, dtype=np.float64)
    total = float(np.sum(np.exp(-taps * taps / SPREAD)))
    i = lax.broadcasted_iota(jnp.int32, (count, count), 0)
    j = lax.broadcasted_iota(jnp.int32, (count, count), 1)
    d = (i - j).astype(f32)
    return jnp.where(jnp.abs(d) <= HALF, jnp.exp(d * d * (-1.0 / SPREAD)), 0.0) * (1.0 / total)


def chip_grid(parts):
    chips = parts // 2
    ny = 2 ** ((chips.bit_length() - 1) // 2)
    return chips // ny, ny


class Links:
    def __init__(self, parts, rows, x_ref, out_ref, a_ref, da_ref, rc, sy, ry, keep, sz, rz, sems):
        self.nz, self.ny = chip_grid(parts)
        self.rows = rows
        self.x_ref, self.out_ref, self.a_ref, self.da_ref = x_ref, out_ref, a_ref, da_ref
        self.rc, self.sy, self.ry, self.keep, self.sz, self.rz = rc, sy, ry, keep, sz, rz
        self.sems = sems
        me = lax.axis_index("atom")
        self.me = me
        self.c = lax.rem(me, 2)
        self.y = lax.rem(me // 2, self.ny)
        self.z = me // (2 * self.ny)
        self.width = a_ref.shape[1] // CHUNKS
        self.sent = []
        self.live = {}

    def index(self, z, y, c):
        return (z * self.ny + y) * 2 + c

    def zp(self, d):
        return lax.rem(self.z + d, self.nz)

    def zm(self, d):
        return lax.rem(self.z + self.nz - d, self.nz)

    def yp(self, d):
        return lax.rem(self.y + d, self.ny)

    def ym(self, d):
        return lax.rem(self.y + self.ny - d, self.ny)

    def barrier(self):
        bar = pltpu.get_barrier_semaphore()
        peers = [self.index(self.z, self.y, 1 - self.c)]
        peers += [self.index(self.zp(d), self.y, self.c) for d in range(1, self.nz)]
        peers += [self.index(self.z, self.yp(d), self.c) for d in range(1, self.ny)]
        for peer in peers:
            pl.semaphore_signal(bar, inc=1, device_id={"atom": peer}, device_id_type=pl.DeviceIdType.MESH)
        pl.semaphore_wait(bar, len(peers))

    def send(self, key, number, src, dst, peer):
        send, recv = self.sems
        copy = pltpu.make_async_remote_copy(
            src_ref=src, dst_ref=dst, send_sem=send.at[number], recv_sem=recv.at[number],
            device_id={"atom": peer}, device_id_type=pl.DeviceIdType.MESH)
        copy.start()
        self.live[key] = copy
        self.sent.append(copy)

    def arrived(self, key):
        self.live[key].wait_recv()

    def finish(self):
        for copy in self.sent:
            copy.wait_send()

    def cols(self, j):
        return pl.ds(j * self.width, self.width)

    def shard(self, index, j):
        return self.a_ref.at[pl.ds(pl.multiple_of(index * self.rows, self.rows), self.rows), self.cols(j)]

    def slots(self):
        return (self.nz - 1) + (self.ny - 1) * self.nz + self.nz * self.ny

    def pass_on(self, what, number, index, j, peer):
        ref = self.shard(index, j)
        self.send((what, number, j), j * self.slots() + number, ref, ref, peer)

    def sibling(self):
        return self.index(self.z, self.y, 1 - self.c)

    def gather_start(self):
        self.a_ref[pl.ds(pl.multiple_of(self.me * self.rows, self.rows), self.rows), :] = self.x_ref[...]
        for j in range(CHUNKS):
            for d in range(1, self.nz):
                self.pass_on("g", d - 1, self.me, j, self.index(self.zp(d), self.y, self.c))
            self.spread(0, j)

    def spread(self, dz, j):
        index = self.index(self.zm(dz), self.y, self.c)
        for dy in range(1, self.ny):
            self.pass_on("g", (self.nz - 1) + (dy - 1) * self.nz + dz, index, j, self.index(self.z, self.yp(dy), self.c))
        self.pass_on("g", (self.nz - 1) + (self.ny - 1) * self.nz + dz, index, j, self.sibling())

    def gather_z(self, j):
        for dz in range(1, self.nz):
            self.arrived(("g", dz - 1, j))
            self.spread(dz, j)

    def gather_y(self, j):
        base = (self.nz - 1) + (self.ny - 1) * self.nz
        for dy in range(1, self.ny):
            for dz in range(self.nz):
                self.arrived(("g", (self.nz - 1) + (dy - 1) * self.nz + dz, j))
                index = self.index(self.zm(dz), self.ym(dy), self.c)
                self.pass_on("g", base + dy * self.nz + dz, index, j, self.sibling())

    def gather_done(self, j):
        base = (self.nz - 1) + (self.ny - 1) * self.nz
        for n in range(self.nz * self.ny):
            self.arrived(("g", base + n, j))

    def number(self, j, slot):
        return CHUNKS * self.slots() + j * (1 + (self.ny - 1) + (self.nz - 1)) + slot

    def reduce_core(self, j):
        cols = self.cols(j)
        self.send(("c", j), self.number(j, 0), self.da_ref.at[:, 1 - self.c, :, cols],
                  self.rc.at[:, :, cols], self.sibling())

    def reduce_y(self, j):
        cols = self.cols(j)
        self.arrived(("c", j))
        for dy in range(self.ny):
            y = self.yp(dy)
            for z in range(self.nz):
                chip = z * self.ny + y
                total = self.da_ref[chip, self.c, :, cols] + self.rc[chip, :, cols]
                if dy == 0:
                    self.keep[z, :, cols] = total
                else:
                    self.sy[dy - 1, z, :, cols] = total
            if dy > 0:
                self.send(("y", dy, j), self.number(j, dy), self.sy.at[dy - 1, :, :, cols],
                          self.ry.at[dy - 1, :, :, cols], self.index(self.z, y, self.c))

    def reduce_z(self, j):
        cols = self.cols(j)
        for dy in range(1, self.ny):
            self.arrived(("y", dy, j))
        for dz in [*range(1, self.nz), 0]:
            z = self.zp(dz)
            total = self.keep[z, :, cols]
            for dy in range(1, self.ny):
                total = total + self.ry[dy - 1, z, :, cols]
            if dz == 0:
                self.out_ref[:, cols] = total
            else:
                self.sz[dz - 1, :, cols] = total
                self.send(("z", dz, j), self.number(j, self.ny - 1 + dz), self.sz.at[dz - 1, :, cols],
                          self.rz.at[dz - 1, :, cols], self.index(z, self.y, self.c))

    def reduce_done(self, j):
        cols = self.cols(j)
        total = self.out_ref[:, cols]
        for dz in range(1, self.nz):
            self.arrived(("z", dz, j))
            total = total + self.rz[dz - 1, :, cols]
        self.out_ref[:, cols] = total


def kernel(H, W, parts, linked, x_ref, y_ref, logit_ref, p_ref, out_ref,
           wc, wr, re_ref, lam, rq1, rq2, rq3, rb2, rb3, u, p1, p2, acc, usum, *rest):
    if linked:
        a_ref, da_ref = rest[:2]
        links = Links(parts, H // parts, x_ref, out_ref, a_ref, da_ref, *rest[2:8], rest[8:10])
        links.barrier()
        links.gather_start()

        def get_da(c):
            return da_ref[:, :, :, c].reshape(H, W)

        def set_da(c, value):
            da_ref[:, :, :, c] = value.reshape(parts // 2, 2, H // parts, W)
    else:
        a_ref = x_ref

        def get_da(c):
            return out_ref[:, c]

        def set_da(c, value):
            out_ref[:, c] = value

    gc = kernel_matrix(W)
    gr = kernel_matrix(H)
    ch, cl = split(gc)
    rh, rl = split(gr)
    wc[:W, :W] = ch
    wc[W:, :W] = ch
    wc[:W, W:] = cl
    wc[W:, W:] = jnp.zeros_like(cl)
    wr[:H, :H] = rh
    wr[:H, H:] = rh
    wr[H:, :H] = rl
    wr[H:, H:] = jnp.zeros_like(rl)
    re_ref[...] = 1.0 / (jnp.sum(gr, axis=1, keepdims=True) * jnp.sum(gc, axis=0, keepdims=True))
    e = jnp.exp(logit_ref[...])
    soft = e / jnp.sum(e, axis=1, keepdims=True)
    for k in range(K):
        lam[:, k * W:(k + 1) * W] = jnp.broadcast_to(soft[:, k:k + 1], (1, W))

    def blur(fields):
        left = []
        for x in fields:
            hi, lo = split(x)
            left.append(jnp.concatenate([hi, lo], axis=1))
        out = jnp.dot(jnp.concatenate(left, axis=0), wc[...], preferred_element_type=f32)
        out = out[:, :W] + out[:, W:]
        right = []
        for n in range(len(fields)):
            hi, lo = split(out[n * H:(n + 1) * H])
            right.append(jnp.concatenate([hi, lo], axis=0))
        out = jnp.dot(wr[...], jnp.concatenate(right, axis=1), preferred_element_type=f32)
        out = out[:H] + out[H:]
        return [out[:, n * W:(n + 1) * W] for n in range(len(fields))]

    def over_slabs(step, begin=0, end=K):
        def one(s, carry):
            step([pl.ds(pl.multiple_of((s * SLAB + n) * W, W), W) for n in range(SLAB)])
            return carry
        lax.fori_loop(begin // SLAB, end // SLAB, one, 0, unroll=True)

    def over_chunk(step, j):
        over_slabs(step, j * K // CHUNKS, (j + 1) * K // CHUNKS)

    def add(total, parts):
        s = parts[0]
        for x in parts[1:]:
            s = s + x
        total[...] += s

    acc[...] = jnp.zeros_like(acc)

    def first(cols):
        q = blur([a_ref[:, c] * re_ref[...] for c in cols])
        for c, x in zip(cols, q):
            rq1[:, c] = 1.0 / x
        add(acc, [lam[:, c] * jnp.log(x) for c, x in zip(cols, q)])
    if linked:
        for t in range(CHUNKS + 2):
            if t < CHUNKS:
                links.gather_z(t)
            if 0 <= t - 1 < CHUNKS:
                links.gather_y(t - 1)
            if t >= 2:
                links.gather_done(t - 2)
                over_chunk(first, t - 2)
    else:
        over_slabs(first)

    def forward(p, rq_in, rb, rq_out):
        p[...] = jnp.exp(acc[...])
        acc[...] = jnp.zeros_like(acc)

        def step(cols):
            b = blur([p[...] * rq_in[:, c] for c in cols])
            r = []
            for c, x in zip(cols, b):
                inv = 1.0 / x
                rb[:, c] = inv
                r.append(a_ref[:, c] * inv)
            q = blur(r)
            for c, x in zip(cols, q):
                rq_out[:, c] = 1.0 / x
            add(acc, [lam[:, c] * jnp.log(x) for c, x in zip(cols, q)])
        over_slabs(step)

    forward(p1, rq1, rb2, rq2)
    forward(p2, rq2, rb3, rq3)
    result = jnp.exp(acc[...])
    p_ref[...] = result
    acc[...] = (y_ref[...] - result) * result

    def backward(p, rq, rb, rq_before, newest):
        usum[...] = acc[...]
        acc[...] = jnp.zeros_like(acc)

        def step(cols):
            dq = []
            for c in cols:
                g = lam[:, c] * usum[...]
                g = -g if newest else u[:, c] - g
                dq.append(g * rq[:, c])
            dr = blur(dq)
            db = []
            for c, x in zip(cols, dr):
                inv = rb[:, c]
                t = x * inv
                set_da(c, t if newest else get_da(c) + t)
                db.append(t * (a_ref[:, c] * inv))
            dv = blur(db)
            parts = []
            for c, x in zip(cols, dv):
                x = x * (p[...] * rq_before[:, c])
                u[:, c] = x
                parts.append(x)
            add(acc, parts)
        over_slabs(step)

    backward(p2, rq3, rb3, rq2, True)
    backward(p1, rq2, rb2, rq1, False)
    usum[...] = acc[...]

    def last(cols):
        d = blur([(u[:, c] - lam[:, c] * usum[...]) * rq1[:, c] for c in cols])
        for c, x in zip(cols, d):
            set_da(c, get_da(c) + x * re_ref[...])
    if linked:
        for t in range(CHUNKS + 3):
            if t < CHUNKS:
                over_chunk(last, t)
                links.reduce_core(t)
            if 0 <= t - 1 < CHUNKS:
                links.reduce_y(t - 1)
            if 0 <= t - 2 < CHUNKS:
                links.reduce_z(t - 2)
            if t >= 3:
                links.reduce_done(t - 3)
        links.finish()
    else:
        over_slabs(last)


def body(atoms, images, logits, *, parts):
    rows, wide = atoms.shape
    H, W = rows * parts, wide // K
    linked = rows % 8 == 0 and images.shape[0] == 1 and parts % 2 == 0
    field = pltpu.VMEM((H, wide), f32)
    plane = pltpu.VMEM((H, W), f32)
    scratch = [
        pltpu.VMEM((2 * W, 2 * W), bf16),
        pltpu.VMEM((2 * H, 2 * H), bf16),
        plane,
        pltpu.VMEM((1, wide), f32),
        field, field, field, field, field, field,
        plane, plane, plane, plane,
    ]
    extra = {}
    if linked:
        nz, ny = chip_grid(parts)
        copies = CHUNKS * ((nz - 1) + (ny - 1) * nz + nz * ny + 1 + (ny - 1) + (nz - 1))
        scratch += [
            field,
            pltpu.VMEM((nz * ny, 2, rows, wide), f32),
            pltpu.VMEM((nz * ny, rows, wide), f32),
            pltpu.VMEM((max(ny - 1, 1), nz, rows, wide), f32),
            pltpu.VMEM((max(ny - 1, 1), nz, rows, wide), f32),
            pltpu.VMEM((nz, rows, wide), f32),
            pltpu.VMEM((max(nz - 1, 1), rows, wide), f32),
            pltpu.VMEM((max(nz - 1, 1), rows, wide), f32),
            pltpu.SemaphoreType.DMA((copies,)),
            pltpu.SemaphoreType.DMA((copies,)),
        ]
        extra = dict(collective_id=0, has_side_effects=True)
    call = pl.pallas_call(
        functools.partial(kernel, H, W, parts, linked),
        out_shape=(
            jax.ShapeDtypeStruct((H, W), f32),
            jax.ShapeDtypeStruct((rows if linked else H, wide), f32),
        ),
        in_specs=[pl.BlockSpec(memory_space=pltpu.VMEM)] * 3,
        out_specs=[pl.BlockSpec(memory_space=pltpu.VMEM)] * 2,
        scratch_shapes=scratch,
        compiler_params=pltpu.CompilerParams(vmem_limit_bytes=44 * 2**20, **extra),
    )
    if linked:
        p, da = call(atoms, images.reshape(H, W), logits)
        return p.reshape(1, H * W), da
    gathered = lax.all_gather(atoms, "atom", axis=0, tiled=True)
    results, grads = [], []
    for n in range(images.shape[0]):
        p, da = call(gathered, images[n].reshape(H, W), logits[n:n + 1])
        results.append(p.reshape(1, H * W))
        grads.append(da)
    result = results[0] if len(results) == 1 else jnp.concatenate(results, axis=0)
    term = sum(grads[1:], grads[0])
    return result, lax.psum_scatter(term, "atom", scatter_dimension=0, tiled=True)


def solution(mesh):
    return jax.shard_map(
        functools.partial(body, parts=mesh.shape["atom"]),
        mesh=mesh,
        in_specs=(P("atom", None), P(("groups", "atom"), None), P(("groups", "atom"), None)),
        out_specs=(P(("groups", "atom"), None), P(("groups", "atom"), None)),
        check_vma=False,
    )
```
